1024 devices in a mesh: seq: 64 (over z, y_lo, core), batch: 16 (over y_hi, x).
Axes of the slice: x: 4, y: 8 (y_hi: 4, y_lo: 2; y = y_hi * 2 + y_lo), z: 16, core: 2. Of those that a mesh axis runs over, the one named last changes fastest.
Arguments:
- inputs: bfloat16 [16, 64, 8192], P('batch'), may hold values from -6 to 6
- w_query: bfloat16 [8192, 8192], P('batch', 'seq'), may hold values from -0.0625 to 0.0625
- cache_keys: bfloat16 [16, 32768, 1024], P('batch', 'seq'), may hold values from -120 to 120
- cache_values: bfloat16 [16, 32768, 1024], P('batch', 'seq'), may hold values from -6 to 6
- lengths: int32 [16], P('batch'), may hold values from 1 to 32768, as said below
- positions: int32 [16, 64], P('batch'), may hold values from 0 to 32767, as said below
Outputs:
- attended: bfloat16 [16, 64, 8192], P('batch', None, 'seq')
The draws below stay inside these ranges and needn't reach their ends.
Inputs may be any that keep to these rules, and one draw needn't show every extreme that they name: `lengths`: every sample has at least one valid position; some sample has all 32768 valid. `positions`: some query sits at position 0 and some at 32767.
All inputs are finite; a program needn't handle non-finite values.
Results may differ from the reference program's by a relative error of at most 0.015.
The reference program's roundings to bfloat16 on the way (of `query`, `prob` and `block_sum`) count: a program that leaves them out, or rounds other values in their place, can miss the bound.
Values may be sent and summed in bfloat16 or wider, within the bound.
A program may use at most 32 MiB of HBM per device.

```python
import jax
import jax.numpy as jnp
from jax import lax

D = 8192
H = 64
KVH = 8
HD = 128
Q = 64
SAMPLES = 16
S = 32768
N_SEQ = 64


def draw_cache_keys(key, part):
    shape = (SAMPLES, S, KVH * HD)
    base = jnp.clip(jax.random.normal(key, shape, jnp.float32), -4.0, 4.0)
    return base.astype(jnp.bfloat16)


def draw_lengths(key, part):
    first, second = jax.random.split(jax.random.fold_in(key, 11))
    drawn = jax.random.randint(first, (SAMPLES,), 1, S + 1)
    which = jax.random.randint(second, (), 0, SAMPLES)
    return drawn.at[which].set(S).astype(jnp.int32)


def draw_positions(key, part):
    drawn = jax.random.randint(jax.random.fold_in(key, 13), (SAMPLES, Q), 0, S)
    drawn = drawn.at[0, 0].set(0).at[SAMPLES - 1, Q - 1].set(S - 1)
    return drawn.astype(jnp.int32)


def steps_of(stream_key, shape, shards, low, high):
    loudness = 1.0
    for position, shards_of in shards:
        draws = jax.random.uniform(jax.random.fold_in(jax.random.fold_in(stream_key, 6), position), (shards_of,), jnp.float32, low / len(shards), high / len(shards))
        loudness = loudness * jnp.repeat(jnp.exp(draws), shape[position] // shards_of).reshape((-1,) + (1,) * (len(shape) - 1 - position))
    return loudness


def bell_draw(rng, shape, scale, reach, shards=(), held_as=jnp.bfloat16):
    level = steps_of(rng, shape, shards, -0.22, 0.18) if shards else 1.0
    array = jax.random.normal(rng, shape, jnp.float32) * scale * level
    return jnp.minimum(jnp.maximum(array, -reach), reach).astype(held_as)


def setup_inputs(seed: int = 0) -> dict:
    key_list = jax.random.split(jax.random.key(seed), 7)
    return {
        "inputs": bell_draw(key_list[0], (SAMPLES, Q, D), 1.0, 6.0, ((0, 16),)),
        "w_query": bell_draw(key_list[1], (D, H * HD), D ** -0.5, 0.0625, ((0, 16), (1, 64))),
        "cache_keys": draw_cache_keys(jax.random.fold_in(key_list[6], 71), 0),
        "cache_values": bell_draw(key_list[3], (SAMPLES, S, KVH * HD), 1.0, 6.0, ((0, 16), (1, 64))),
        "lengths": draw_lengths(jax.random.fold_in(key_list[6], 71), 0),
        "positions": draw_positions(jax.random.fold_in(key_list[6], 71), 0),
    }


def one_sample(w_query, args):
    tokens, key_rows, value_rows, length, place = args
    group = H // KVH
    block_len = S // N_SEQ
    query = jnp.dot(tokens, w_query, preferred_element_type=jnp.float32).astype(jnp.bfloat16)
    query_heads = query.reshape(Q, KVH, group, HD).astype(jnp.float32)
    key_blocks = key_rows.reshape(N_SEQ, block_len, KVH, HD)
    value_blocks = value_rows.reshape(N_SEQ, block_len, KVH, HD)

    def one_block(items):
        key_block, value_block, index = items
        key_pos = index * block_len + jnp.arange(block_len, dtype=jnp.int32)
        visible = (key_pos[None, :] <= place[:, None]) & (key_pos[None, :] < length)
        score = jnp.einsum('qgrd,kgd->grqk', query_heads, key_block.astype(jnp.float32)) * (HD ** -0.5)
        block_max = jnp.max(jnp.where(visible, score, -1e30), axis=-1)
        expo = jnp.where(visible, jnp.exp(score - block_max[..., None]), 0.0)
        block_total = jnp.sum(expo, axis=-1)
        prob = expo.astype(jnp.bfloat16).astype(jnp.float32)
        block_sum = jnp.einsum('grqk,kgd->grqd', prob, value_block.astype(jnp.float32)).astype(jnp.bfloat16)
        return block_sum.reshape(H, Q, HD), block_max.reshape(H, Q), block_total.reshape(H, Q)

    sums, maxima, totals = lax.map(one_block, (key_blocks, value_blocks, jnp.arange(N_SEQ, dtype=jnp.int32)))
    top = jnp.max(maxima, axis=0)
    weight = jnp.exp(maxima - top[None])
    numer = jnp.sum(weight[..., None] * sums.astype(jnp.float32), axis=0)
    denom = jnp.sum(weight * totals, axis=0)
    result = numer / denom[..., None]
    return jnp.transpose(result, (1, 0, 2)).reshape(Q, H * HD).astype(jnp.bfloat16)


def reference(inputs, w_query, cache_keys, cache_values, lengths, positions):
    def per_sample(args):
        return one_sample(w_query, args)

    return lax.map(per_sample, (inputs, cache_keys, cache_values, lengths, positions))
```

```python
import functools
import jax
import jax.numpy as jnp
from jax import lax
from jax.experimental import pallas as pl
from jax.experimental.pallas import tpu as pltpu
from jax.sharding import PartitionSpec as P

MESH = pl.DeviceIdType.MESH
HD = 128
QUAD = 4
NX = 4
NYH = 4
NZ = 16
UNITS = 4
ROWS = 64
DEPTH = 512
KEYS = 512
PAY = ROWS + 16
SCALE = HD ** (-0.5) * 1.4426950408889634
NEG = -1e30


def arrived(ref, sem):
    pltpu.make_async_copy(ref, ref, sem).wait()


def kernel(
    x_ref, w_ref, k_ref, v_ref, len_ref, pos_ref, o_ref,
    wbuf, xbuf, part, pbuf, qown, qbuf, kbuf, vbuf, bias, sbuf, outb, inb, coef,
    w_send, w_recv, x_send, x_recv, kv_send, kv_recv, p_send, p_recv, q_send, q_recv, o_send, o_recv,
):
    s = lax.axis_index("seq")
    b = lax.axis_index("batch")
    z, quad = s // QUAD, s % QUAD
    yh, x = b // NX, b % NX
    unit_of_me = 2 * (z // 8) + z % 2
    handler = (z // 2) % QUAD

    def at_seq(t):
        return {"seq": t, "batch": b}

    def at_batch(t):
        return {"seq": s, "batch": t}

    def z_of_unit(u):
        return 2 * quad + 8 * (u // 2) + u % 2

    def piece(j, xt):
        return x_ref.at[0, :, pl.ds(pl.multiple_of((j * NX + xt) * DEPTH, DEPTH), DEPTH)]

    def k_cols(g):
        return k_ref.at[0, :, pl.ds(pl.multiple_of(g * HD, HD), HD)]

    def v_cols(g):
        return v_ref.at[0, :, pl.ds(pl.multiple_of(g * HD, HD), HD)]

    mine = pl.ds(pl.multiple_of(quad * KEYS, KEYS), KEYS)

    pltpu.make_async_copy(w_ref, wbuf.at[yh], w_recv.at[yh]).start()
    for j in range(NYH):
        pltpu.make_async_copy(piece(j, x), xbuf.at[j, pl.ds(x * ROWS, ROWS)], x_recv.at[x * NYH + j]).start()
    for a in range(2):
        g = quad + QUAD * a
        pltpu.make_async_copy(k_cols(g), kbuf.at[a, mine], kv_recv.at[quad * 4 + a]).start()
        pltpu.make_async_copy(v_cols(g), vbuf.at[a, mine], kv_recv.at[quad * 4 + 2 + a]).start()

    barrier = pltpu.get_barrier_semaphore()

    def greet(t):
        pl.semaphore_signal(barrier, inc=1, device_id=t, device_id_type=MESH)

    for d in range(1, NYH):
        greet(at_batch(lax.rem(yh + d, NYH) * NX + x))
    for d in range(1, NX):
        greet(at_batch(yh * NX + lax.rem(x + d, NX)))
    for d in range(1, QUAD):
        greet(at_seq(z * QUAD + lax.rem(quad + d, QUAD)))

    def greet_z(i, carry):
        t = i * QUAD + handler
        u = i // QUAD
        owner = z_of_unit(u) * QUAD + i % QUAD

        @pl.when(t != s)
        def _():
            greet(at_seq(t))

        @pl.when(owner != s)
        def _():
            greet(at_seq(owner))

        return carry

    lax.fori_loop(0, NZ, greet_z, 0)

    lane = lax.broadcasted_iota(jnp.int32, (1, 2 * ROWS), 1)
    pos = pos_ref[...]
    last = jnp.minimum(jnp.concatenate([pos, pos], axis=1) + 1, len_ref[0])

    def fill_bias(i, carry):
        row = lax.broadcasted_iota(jnp.int32, (128, 2 * ROWS), 0) + (z * QUAD * KEYS + i * 128)
        bias[pl.ds(pl.multiple_of(i * 128, 128), 128), :] = jnp.where(row < last, 0.0, NEG)
        return carry

    lax.fori_loop(0, QUAD * KEYS // 128, fill_bias, 0)

    self_handled = (handler == quad).astype(jnp.int32)
    pl.semaphore_wait(barrier, 2 * NZ + 9 - 2 * self_handled)

    copies = []
    for d in (2, 1, 3):
        t = lax.rem(yh + d, NYH)
        copies.append(pltpu.make_async_remote_copy(
            src_ref=w_ref, dst_ref=wbuf.at[yh], send_sem=w_send.at[d], recv_sem=w_recv.at[yh],
            device_id=at_batch(t * NX + x), device_id_type=MESH))
        copies[-1].start()
        t = lax.rem(x + d, NX)
        for j in range(NYH):
            copies.append(pltpu.make_async_remote_copy(
                src_ref=piece(j, t), dst_ref=xbuf.at[j, pl.ds(x * ROWS, ROWS)],
                send_sem=x_send.at[d * NYH + j], recv_sem=x_recv.at[x * NYH + j],
                device_id=at_batch(yh * NX + t), device_id_type=MESH))
            copies[-1].start()

    for a in range(2):
        for d in range(1, QUAD):
            h = lax.rem(quad + d, QUAD)
            g = h + QUAD * a
            for what, (cols, buf) in enumerate(((k_cols, kbuf), (v_cols, vbuf))):
                copies.append(pltpu.make_async_remote_copy(
                    src_ref=cols(g), dst_ref=buf.at[a, mine],
                    send_sem=kv_send.at[d * 4 + what * 2 + a], recv_sem=kv_recv.at[quad * 4 + what * 2 + a],
                    device_id=at_seq(z * QUAD + h), device_id_type=MESH))
                copies[-1].start()

    for d in range(NYH):
        j = lax.rem(yh + d, NYH)
        arrived(wbuf.at[j], w_recv.at[j])
        for t in range(NX):
            arrived(xbuf.at[j, pl.ds(t * ROWS, ROWS)], x_recv.at[t * NYH + j])
        term = jnp.dot(xbuf[j], wbuf[j], preferred_element_type=jnp.float32)
        if d == 0:
            part[...] = term
        else:
            part[...] += term
    for d in (2, 1, 3):
        t = lax.rem(x + d, NX)
        copies.append(pltpu.make_async_remote_copy(
            src_ref=part.at[pl.ds(t * ROWS, ROWS)], dst_ref=pbuf.at[x],
            send_sem=p_send.at[d], recv_sem=p_recv.at[x],
            device_id=at_batch(yh * NX + t), device_id_type=MESH))
        copies[-1].start()
    pltpu.make_async_copy(part.at[pl.ds(x * ROWS, ROWS)], pbuf.at[x], p_recv.at[x]).start()
    for t in range(NX):
        arrived(pbuf.at[t], p_recv.at[t])
    qown[...] = (pbuf[0] + pbuf[1] + pbuf[2] + pbuf[3]).astype(jnp.bfloat16)

    my_rows = pl.ds(pl.multiple_of(quad * ROWS, ROWS), ROWS)
    q_slot = unit_of_me * QUAD + quad

    def q_copy(i):
        t = lax.rem(z + NZ // 2 + i, NZ) * QUAD + handler
        return t, pltpu.make_async_remote_copy(
            src_ref=qown, dst_ref=qbuf.at[unit_of_me, my_rows], send_sem=q_send.at[i], recv_sem=q_recv.at[q_slot],
            device_id=at_seq(t), device_id_type=MESH)

    def send_q(i, carry):
        t, copy = q_copy(i)

        @pl.when(t != s)
        def _():
            copy.start()

        @pl.when(t == s)
        def _():
            pltpu.make_async_copy(qown, qbuf.at[unit_of_me, my_rows], q_recv.at[q_slot]).start()

        return carry

    lax.fori_loop(0, NZ, send_q, 0)

    def o_copy(u, r):
        t = z_of_unit(u) * QUAD + r
        return t, pltpu.make_async_remote_copy(
            src_ref=outb.at[u, r], dst_ref=inb.at[z], send_sem=o_send.at[u * QUAD + r], recv_sem=o_recv.at[z],
            device_id=at_seq(t), device_id_type=MESH)

    width = QUAD * ROWS

    def attend(u, carry):
        a = u // 2

        @pl.when(u % 2 == 0)
        def _():
            for src in range(QUAD):
                part_rows = pl.ds(src * KEYS, KEYS)
                arrived(kbuf.at[a, part_rows], kv_recv.at[src * 4 + a])
                arrived(vbuf.at[a, part_rows], kv_recv.at[src * 4 + 2 + a])

        for r in range(QUAD):
            arrived(qbuf.at[u, pl.ds(r * ROWS, ROWS)], q_recv.at[u * QUAD + r])
        query = qbuf[u]

        def scores(c, top):
            rows = pl.ds(pl.multiple_of(c * KEYS, KEYS), KEYS)
            raw = lax.dot_general(
                kbuf[a, rows, :], query, (((1,), (1,)), ((), ())), preferred_element_type=jnp.float32
            )
            add = bias[rows, :]
            val = raw * SCALE + jnp.concatenate([add, add], axis=1)
            sbuf[rows, :] = val
            return jnp.maximum(top, jnp.max(val.reshape(KEYS // 8, 8, width), axis=0))

        top = lax.fori_loop(0, QUAD, scores, jnp.full((8, width), -3e38, jnp.float32))
        top = jnp.max(top, axis=0, keepdims=True)

        def weigh(c, carry):
            total, acc = carry
            rows = pl.ds(pl.multiple_of(c * KEYS, KEYS), KEYS)
            expo = jnp.exp2(sbuf[rows, :] - top)
            total = total + jnp.sum(expo.reshape(KEYS // 8, 8, width), axis=0)
            acc = acc + lax.dot_general(
                vbuf[a, rows, :], expo.astype(jnp.bfloat16), (((0,), (0,)), ((), ())),
                preferred_element_type=jnp.float32,
            )
            return total, acc

        total, acc = lax.fori_loop(
            0, QUAD, weigh,
            (jnp.zeros((8, width), jnp.float32), jnp.zeros((HD, width), jnp.float32)),
        )
        total = jnp.sum(total, axis=0, keepdims=True)

        def three(val):
            hi = val.astype(jnp.bfloat16).astype(jnp.float32)
            mid = (val - hi).astype(jnp.bfloat16).astype(jnp.float32)
            return hi, mid, val - hi - mid

        sub = lax.broadcasted_iota(jnp.int32, (16, width), 0)
        stats = jnp.zeros((16, width), jnp.float32)
        for i, val in enumerate(three(top) + three(total)):
            stats = jnp.where(sub == i, val, stats)
        stats = stats.astype(jnp.bfloat16)
        for half in range(2):
            block = acc[:, half * 128:(half + 1) * 128].T.astype(jnp.bfloat16)
            for r in range(2):
                slot = outb.at[u, half * 2 + r]
                slot[pl.ds(0, ROWS), :] = block[r * ROWS:(r + 1) * ROWS]
                slot[pl.ds(ROWS, 16), :] = stats[:, half * 128:(half + 1) * 128]
        for r in range(QUAD):
            t, copy = o_copy(u, r)

            @pl.when(t != s)
            def _():
                copy.start()

            @pl.when(t == s)
            def _():
                pltpu.make_async_copy(outb.at[u, r], inb.at[z], o_recv.at[z]).start()

        return carry

    lax.fori_loop(0, UNITS, attend, 0)

    for i in range(NZ):
        arrived(inb.at[i], o_recv.at[i])
    maxima, totals = [], []
    for i in range(NZ):
        st = inb[i, pl.ds(ROWS, 16), :].astype(jnp.float32)
        maxima.append(st[0:1] + st[1:2] + st[2:3])
        totals.append(st[3:4] + st[4:5] + st[5:6])
    top = functools.reduce(jnp.maximum, maxima)
    weights = [jnp.exp2(m - top) for m in maxima]
    denom = functools.reduce(jnp.add, [w * t for w, t in zip(weights, totals)])
    inverse = 1.0 / denom
    sub = lax.broadcasted_iota(jnp.int32, (128, 128), 0)
    table = jnp.zeros((128, 128), jnp.float32)
    for i in range(NZ):
        table = jnp.where(sub == i, weights[i] * inverse, table)
    coef[...] = table.T
    mine_rows = pl.ds(pl.multiple_of((quad % 2) * ROWS, ROWS), ROWS)
    cols = coef[mine_rows, :]
    result = jnp.zeros((ROWS, HD), jnp.float32)
    for i in range(NZ):
        result = result + cols[:, i:i + 1] * inb[i, pl.ds(0, ROWS), :].astype(jnp.float32)
    o_ref[0] = result.astype(jnp.bfloat16)

    for copy in copies:
        copy.wait_send()

    def left(i, carry):
        t, copy = q_copy(i)

        @pl.when(t != s)
        def _():
            copy.wait_send()

        t2, copy2 = o_copy(i // QUAD, i % QUAD)

        @pl.when(t2 != s)
        def _():
            copy2.wait_send()

        return carry

    lax.fori_loop(0, NZ, left, 0)


def on_device(inputs, w_query, cache_keys, cache_values, lengths, positions):
    any_spec = pl.BlockSpec(memory_space=pl.ANY)
    bf, f32 = jnp.bfloat16, jnp.float32
    dma = pltpu.SemaphoreType.DMA
    return pl.pallas_call(
        kernel,
        out_shape=jax.ShapeDtypeStruct((1, ROWS, HD), bf),
        in_specs=[any_spec] * 4 + [pl.BlockSpec(memory_space=pltpu.SMEM), pl.BlockSpec(memory_space=pltpu.VMEM)],
        out_specs=pl.BlockSpec(memory_space=pltpu.VMEM),
        scratch_shapes=[
            pltpu.VMEM((NYH, DEPTH, HD), bf),
            pltpu.VMEM((NYH, NX * ROWS, DEPTH), bf),
            pltpu.VMEM((NX * ROWS, HD), f32),
            pltpu.VMEM((NX, ROWS, HD), f32),
            pltpu.VMEM((ROWS, HD), bf),
            pltpu.VMEM((UNITS, QUAD * ROWS, HD), bf),
            pltpu.VMEM((2, QUAD * KEYS, HD), bf),
            pltpu.VMEM((2, QUAD * KEYS, HD), bf),
            pltpu.VMEM((QUAD * KEYS, 2 * ROWS), f32),
            pltpu.VMEM((QUAD * KEYS, QUAD * ROWS), f32),
            pltpu.VMEM((UNITS, QUAD, PAY, HD), bf),
            pltpu.VMEM((NZ, PAY, HD), bf),
            pltpu.VMEM((128, 128), f32),
            dma((NYH,)), dma((NYH,)),
            dma((NX * NYH,)), dma((NX * NYH,)),
            dma((QUAD * 4,)), dma((QUAD * 4,)),
            dma((NX,)), dma((NX,)),
            dma((NZ,)), dma((NZ,)),
            dma((NZ,)), dma((NZ,)),
        ],
        compiler_params=pltpu.CompilerParams(
            collective_id=0, has_side_effects=True, vmem_limit_bytes=40 * 2**20
        ),
    )(inputs, w_query, cache_keys, cache_values, lengths, positions)


def solution(mesh):
    in_specs = (
        P("batch", None, None),
        P("batch", "seq"),
        P("batch", "seq", None),
        P("batch", "seq", None),
        P("batch"),
        P("batch", None),
    )
    return jax.shard_map(
        on_device, mesh=mesh, in_specs=in_specs, out_specs=P("batch", None, "seq"), check_vma=False
    )
```

```python
import functools
import jax
import jax.numpy as jnp
from jax import lax
from jax.experimental import pallas as pl
from jax.experimental.pallas import tpu as pltpu
from jax.sharding import PartitionSpec as P

MESH = pl.DeviceIdType.MESH
HD = 128
QUAD = 4
NX = 4
NYH = 4
NZ = 16
UNITS = 4
ROWS = 64
DEPTH = 512
KEYS = 512
PAY = ROWS + 16
SCALE = HD ** (-0.5) * 1.4426950408889634
NEG = -1e30


def arrived(ref, sem):
    pltpu.make_async_copy(ref, ref, sem).wait()


def kernel(
    x_ref, w_ref, k_ref, v_ref, len_ref, pos_ref, o_ref,
    wbuf, xbuf, part, pbuf, qown, qbuf, kbuf, vbuf, bias, sbuf, outb, inb, coef,
    w_send, w_recv, x_send, x_recv, kv_send, kv_recv, p_send, p_recv, q_send, q_recv, o_send, o_recv,
    plane_sem, group_sem,
):
    s = lax.axis_index("seq")
    b = lax.axis_index("batch")
    z, quad = s // QUAD, s % QUAD
    yh, x = b // NX, b % NX
    unit_of_me = 2 * (z // 8) + z % 2
    handler = (z // 2) % QUAD

    def at_seq(t):
        return {"seq": t, "batch": b}

    def at_batch(t):
        return {"seq": s, "batch": t}

    def z_of_unit(u):
        return 2 * quad + 8 * (u // 2) + u % 2

    def piece(j, xt):
        return x_ref.at[0, :, pl.ds(pl.multiple_of((j * NX + xt) * DEPTH, DEPTH), DEPTH)]

    def k_cols(g):
        return k_ref.at[0, :, pl.ds(pl.multiple_of(g * HD, HD), HD)]

    def v_cols(g):
        return v_ref.at[0, :, pl.ds(pl.multiple_of(g * HD, HD), HD)]

    mine = pl.ds(pl.multiple_of(quad * KEYS, KEYS), KEYS)

    pltpu.make_async_copy(w_ref, wbuf.at[yh], w_recv.at[yh]).start()
    for j in range(NYH):
        pltpu.make_async_copy(piece(j, x), xbuf.at[j, pl.ds(x * ROWS, ROWS)], x_recv.at[x * NYH + j]).start()
    for a in range(2):
        g = quad + QUAD * a
        pltpu.make_async_copy(k_cols(g), kbuf.at[a, mine], kv_recv.at[quad * 4 + a]).start()
        pltpu.make_async_copy(v_cols(g), vbuf.at[a, mine], kv_recv.at[quad * 4 + 2 + a]).start()

    barrier = pltpu.get_barrier_semaphore()

    def greet(t):
        pl.semaphore_signal(barrier, inc=1, device_id=t, device_id_type=MESH)

    watch = QUAD - 1
    stand_in = jnp.where(quad == watch, s - 1, s)
    for d in range(1, NYH):
        greet({"seq": stand_in, "batch": lax.rem(yh + d, NYH) * NX + x})
    for d in range(1, NX):
        greet({"seq": stand_in, "batch": yh * NX + lax.rem(x + d, NX)})
    for q in range(QUAD - 1):
        @pl.when(q != quad)
        def _():
            greet(at_seq(z * QUAD + q))

    def greet_z(i, carry):
        t = lax.rem(z + i, NZ) * QUAD + watch

        @pl.when(t != s)
        def _():
            greet(at_seq(t))

        return carry

    lax.fori_loop(0, NZ, greet_z, 0)

    lane = lax.broadcasted_iota(jnp.int32, (1, 2 * ROWS), 1)
    pos = pos_ref[...]
    last = jnp.minimum(jnp.concatenate([pos, pos], axis=1) + 1, len_ref[0])

    def fill_bias(i, carry):
        row = lax.broadcasted_iota(jnp.int32, (128, 2 * ROWS), 0) + (z * QUAD * KEYS + i * 128)
        bias[pl.ds(pl.multiple_of(i * 128, 128), 128), :] = jnp.where(row < last, 0.0, NEG)
        return carry

    lax.fori_loop(0, QUAD * KEYS // 128, fill_bias, 0)

    @pl.when(quad < watch - 1)
    def _():
        pl.semaphore_wait(barrier, 9)

    @pl.when(quad == watch - 1)
    def _():
        pl.semaphore_wait(barrier, 15)
        pl.semaphore_signal(plane_sem, inc=1, device_id=at_seq(s + 1), device_id_type=MESH)

    @pl.when(quad == watch)
    def _():
        pl.semaphore_wait(plane_sem, 1)

    copies = []
    for d in (2, 1, 3):
        t = lax.rem(yh + d, NYH)
        copies.append(pltpu.make_async_remote_copy(
            src_ref=w_ref, dst_ref=wbuf.at[yh], send_sem=w_send.at[d], recv_sem=w_recv.at[yh],
            device_id=at_batch(t * NX + x), device_id_type=MESH))
        copies[-1].start()
        t = lax.rem(x + d, NX)
        for j in range(NYH):
            copies.append(pltpu.make_async_remote_copy(
                src_ref=piece(j, t), dst_ref=xbuf.at[j, pl.ds(x * ROWS, ROWS)],
                send_sem=x_send.at[d * NYH + j], recv_sem=x_recv.at[x * NYH + j],
                device_id=at_batch(yh * NX + t), device_id_type=MESH))
            copies[-1].start()

    for a in range(2):
        for d in range(1, QUAD):
            h = lax.rem(quad + d, QUAD)
            g = h + QUAD * a
            for what, (cols, buf) in enumerate(((k_cols, kbuf), (v_cols, vbuf))):
                copies.append(pltpu.make_async_remote_copy(
                    src_ref=cols(g), dst_ref=buf.at[a, mine],
                    send_sem=kv_send.at[d * 4 + what * 2 + a], recv_sem=kv_recv.at[quad * 4 + what * 2 + a],
                    device_id=at_seq(z * QUAD + h), device_id_type=MESH))
                copies[-1].start()

    for d in range(NYH):
        j = lax.rem(yh + d, NYH)
        arrived(wbuf.at[j], w_recv.at[j])
        for t in range(NX):
            arrived(xbuf.at[j, pl.ds(t * ROWS, ROWS)], x_recv.at[t * NYH + j])
        term = jnp.dot(xbuf[j], wbuf[j], preferred_element_type=jnp.float32)
        if d == 0:
            part[...] = term
        else:
            part[...] += term
    for d in (2, 1, 3):
        t = lax.rem(x + d, NX)
        copies.append(pltpu.make_async_remote_copy(
            src_ref=part.at[pl.ds(t * ROWS, ROWS)], dst_ref=pbuf.at[x],
            send_sem=p_send.at[d], recv_sem=p_recv.at[x],
            device_id=at_batch(yh * NX + t), device_id_type=MESH))
        copies[-1].start()
    pltpu.make_async_copy(part.at[pl.ds(x * ROWS, ROWS)], pbuf.at[x], p_recv.at[x]).start()

    @pl.when(quad == watch)
    def _():
        pl.semaphore_wait(barrier, NZ * QUAD - 1)
        for d in range(1, QUAD):
            pl.semaphore_signal(group_sem, inc=1, device_id=at_seq(s - d), device_id_type=MESH)

    for t in range(NX):
        arrived(pbuf.at[t], p_recv.at[t])
    qown[...] = (pbuf[0] + pbuf[1] + pbuf[2] + pbuf[3]).astype(jnp.bfloat16)

    @pl.when(quad != watch)
    def _():
        pl.semaphore_wait(group_sem, 1)

    my_rows = pl.ds(pl.multiple_of(quad * ROWS, ROWS), ROWS)
    q_slot = unit_of_me * QUAD + quad

    def q_copy(i):
        t = lax.rem(z + NZ // 2 + i, NZ) * QUAD + handler
        return t, pltpu.make_async_remote_copy(
            src_ref=qown, dst_ref=qbuf.at[unit_of_me, my_rows], send_sem=q_send.at[i], recv_sem=q_recv.at[q_slot],
            device_id=at_seq(t), device_id_type=MESH)

    def send_q(i, carry):
        t, copy = q_copy(i)

        @pl.when(t != s)
        def _():
            copy.start()

        @pl.when(t == s)
        def _():
            pltpu.make_async_copy(qown, qbuf.at[unit_of_me, my_rows], q_recv.at[q_slot]).start()

        return carry

    lax.fori_loop(0, NZ, send_q, 0)

    def o_copy(u, r):
        t = z_of_unit(u) * QUAD + r
        return t, pltpu.make_async_remote_copy(
            src_ref=outb.at[u, r], dst_ref=inb.at[z], send_sem=o_send.at[u * QUAD + r], recv_sem=o_recv.at[z],
            device_id=at_seq(t), device_id_type=MESH)

    width = QUAD * ROWS

    def attend(u, carry):
        a = u // 2

        @pl.when(u % 2 == 0)
        def _():
            for src in range(QUAD):
                part_rows = pl.ds(src * KEYS, KEYS)
                arrived(kbuf.at[a, part_rows], kv_recv.at[src * 4 + a])
                arrived(vbuf.at[a, part_rows], kv_recv.at[src * 4 + 2 + a])

        for r in range(QUAD):
            arrived(qbuf.at[u, pl.ds(r * ROWS, ROWS)], q_recv.at[u * QUAD + r])
        query = qbuf[u]

        def scores(c, top):
            rows = pl.ds(pl.multiple_of(c * KEYS, KEYS), KEYS)
            raw = lax.dot_general(
                kbuf[a, rows, :], query, (((1,), (1,)), ((), ())), preferred_element_type=jnp.float32
            )
            add = bias[rows, :]
            val = raw * SCALE + jnp.concatenate([add, add], axis=1)
            sbuf[rows, :] = val
            return jnp.maximum(top, jnp.max(val.reshape(KEYS // 8, 8, width), axis=0))

        top = lax.fori_loop(0, QUAD, scores, jnp.full((8, width), -3e38, jnp.float32))
        top = jnp.max(top, axis=0, keepdims=True)

        def weigh(c, carry):
            total, acc = carry
            rows = pl.ds(pl.multiple_of(c * KEYS, KEYS), KEYS)
            expo = jnp.exp2(sbuf[rows, :] - top)
            total = total + jnp.sum(expo.reshape(KEYS // 8, 8, width), axis=0)
            acc = acc + lax.dot_general(
                vbuf[a, rows, :], expo.astype(jnp.bfloat16), (((0,), (0,)), ((), ())),
                preferred_element_type=jnp.float32,
            )
            return total, acc

        total, acc = lax.fori_loop(
            0, QUAD, weigh,
            (jnp.zeros((8, width), jnp.float32), jnp.zeros((HD, width), jnp.float32)),
        )
        total = jnp.sum(total, axis=0, keepdims=True)

        def three(val):
            hi = val.astype(jnp.bfloat16).astype(jnp.float32)
            mid = (val - hi).astype(jnp.bfloat16).astype(jnp.float32)
            return hi, mid, val - hi - mid

        sub = lax.broadcasted_iota(jnp.int32, (16, width), 0)
        stats = jnp.zeros((16, width), jnp.float32)
        for i, val in enumerate(three(top) + three(total)):
            stats = jnp.where(sub == i, val, stats)
        stats = stats.astype(jnp.bfloat16)
        for half in range(2):
            block = acc[:, half * 128:(half + 1) * 128].T.astype(jnp.bfloat16)
            for r in range(2):
                slot = outb.at[u, half * 2 + r]
                slot[pl.ds(0, ROWS), :] = block[r * ROWS:(r + 1) * ROWS]
                slot[pl.ds(ROWS, 16), :] = stats[:, half * 128:(half + 1) * 128]
        for r in range(QUAD):
            t, copy = o_copy(u, r)

            @pl.when(t != s)
            def _():
                copy.start()

            @pl.when(t == s)
            def _():
                pltpu.make_async_copy(outb.at[u, r], inb.at[z], o_recv.at[z]).start()

        return carry

    lax.fori_loop(0, UNITS, attend, 0)

    for i in range(NZ):
        arrived(inb.at[i], o_recv.at[i])
    maxima, totals = [], []
    for i in range(NZ):
        st = inb[i, pl.ds(ROWS, 16), :].astype(jnp.float32)
        maxima.append(st[0:1] + st[1:2] + st[2:3])
        totals.append(st[3:4] + st[4:5] + st[5:6])
    top = functools.reduce(jnp.maximum, maxima)
    weights = [jnp.exp2(m - top) for m in maxima]
    denom = functools.reduce(jnp.add, [w * t for w, t in zip(weights, totals)])
    inverse = 1.0 / denom
    sub = lax.broadcasted_iota(jnp.int32, (128, 128), 0)
    table = jnp.zeros((128, 128), jnp.float32)
    for i in range(NZ):
        table = jnp.where(sub == i, weights[i] * inverse, table)
    coef[...] = table.T
    mine_rows = pl.ds(pl.multiple_of((quad % 2) * ROWS, ROWS), ROWS)
    cols = coef[mine_rows, :]
    result = jnp.zeros((ROWS, HD), jnp.float32)
    for i in range(NZ):
        result = result + cols[:, i:i + 1] * inb[i, pl.ds(0, ROWS), :].astype(jnp.float32)
    o_ref[0] = result.astype(jnp.bfloat16)

    for copy in copies:
        copy.wait_send()

    def left(i, carry):
        t, copy = q_copy(i)

        @pl.when(t != s)
        def _():
            copy.wait_send()

        t2, copy2 = o_copy(i // QUAD, i % QUAD)

        @pl.when(t2 != s)
        def _():
            copy2.wait_send()

        return carry

    lax.fori_loop(0, NZ, left, 0)


def on_device(inputs, w_query, cache_keys, cache_values, lengths, positions):
    any_spec = pl.BlockSpec(memory_space=pl.ANY)
    bf, f32 = jnp.bfloat16, jnp.float32
    dma = pltpu.SemaphoreType.DMA
    return pl.pallas_call(
        kernel,
        out_shape=jax.ShapeDtypeStruct((1, ROWS, HD), bf),
        in_specs=[any_spec] * 4 + [pl.BlockSpec(memory_space=pltpu.SMEM), pl.BlockSpec(memory_space=pltpu.VMEM)],
        out_specs=pl.BlockSpec(memory_space=pltpu.VMEM),
        scratch_shapes=[
            pltpu.VMEM((NYH, DEPTH, HD), bf),
            pltpu.VMEM((NYH, NX * ROWS, DEPTH), bf),
            pltpu.VMEM((NX * ROWS, HD), f32),
            pltpu.VMEM((NX, ROWS, HD), f32),
            pltpu.VMEM((ROWS, HD), bf),
            pltpu.VMEM((UNITS, QUAD * ROWS, HD), bf),
            pltpu.VMEM((2, QUAD * KEYS, HD), bf),
            pltpu.VMEM((2, QUAD * KEYS, HD), bf),
            pltpu.VMEM((QUAD * KEYS, 2 * ROWS), f32),
            pltpu.VMEM((QUAD * KEYS, QUAD * ROWS), f32),
            pltpu.VMEM((UNITS, QUAD, PAY, HD), bf),
            pltpu.VMEM((NZ, PAY, HD), bf),
            pltpu.VMEM((128, 128), f32),
            dma((NYH,)), dma((NYH,)),
            dma((NX * NYH,)), dma((NX * NYH,)),
            dma((QUAD * 4,)), dma((QUAD * 4,)),
            dma((NX,)), dma((NX,)),
            dma((NZ,)), dma((NZ,)),
            dma((NZ,)), dma((NZ,)),
            pltpu.SemaphoreType.REGULAR, pltpu.SemaphoreType.REGULAR,
        ],
        compiler_params=pltpu.CompilerParams(
            collective_id=0, has_side_effects=True, vmem_limit_bytes=40 * 2**20
        ),
    )(inputs, w_query, cache_keys, cache_values, lengths, positions)


def solution(mesh):
    in_specs = (
        P("batch", None, None),
        P("batch", "seq"),
        P("batch", "seq", None),
        P("batch", "seq", None),
        P("batch"),
        P("batch", None),
    )
    return jax.shard_map(
        on_device, mesh=mesh, in_specs=in_specs, out_specs=P("batch", None, "seq"), check_vma=False
    )
```

```python
import functools
import jax
import jax.numpy as jnp
from jax import lax
from jax.experimental import pallas as pl
from jax.experimental.pallas import tpu as pltpu
from jax.sharding import PartitionSpec as P

MESH = pl.DeviceIdType.MESH
HD = 128
QUAD = 4
NX = 4
NYH = 4
NZ = 16
UNITS = 4
ROWS = 64
DEPTH = 512
KEYS = 512
SCALE = HD ** (-0.5) * 1.4426950408889634
NEG = -1e30


def arrived(ref, sem):
    pltpu.make_async_copy(ref, ref, sem).wait()


def kernel(
    x_ref, w_ref, k_ref, v_ref, len_ref, pos_ref, o_ref,
    wbuf, xbuf, part, pbuf, qown, qbuf, kbuf, vbuf, bias, sbuf, outb, inb, outs, ins, coef,
    w_send, w_recv, x_send, x_recv, kv_send, kv_recv, p_send, p_recv, q_send, q_recv, o_send, o_recv, t_send, t_recv,
    plane_sem, group_sem,
):
    s = lax.axis_index("seq")
    b = lax.axis_index("batch")
    z, quad = s // QUAD, s % QUAD
    yh, x = b // NX, b % NX
    unit_of_me = 2 * (z // 8) + z % 2
    handler = (z // 2) % QUAD

    def at_seq(t):
        return {"seq": t, "batch": b}

    def at_batch(t):
        return {"seq": s, "batch": t}

    def z_of_unit(u):
        return 2 * quad + 8 * (u // 2) + u % 2

    def piece(j, xt):
        return x_ref.at[0, :, pl.ds(pl.multiple_of((j * NX + xt) * DEPTH, DEPTH), DEPTH)]

    def k_cols(g):
        return k_ref.at[0, :, pl.ds(pl.multiple_of(g * HD, HD), HD)]

    def v_cols(g):
        return v_ref.at[0, :, pl.ds(pl.multiple_of(g * HD, HD), HD)]

    mine = pl.ds(pl.multiple_of(quad * KEYS, KEYS), KEYS)

    pltpu.make_async_copy(w_ref, wbuf.at[yh], w_recv.at[yh]).start()
    for j in range(NYH):
        pltpu.make_async_copy(piece(j, x), xbuf.at[j, pl.ds(x * ROWS, ROWS)], x_recv.at[x * NYH + j]).start()
    for a in range(2):
        g = quad + QUAD * a
        pltpu.make_async_copy(k_cols(g), kbuf.at[a, mine], kv_recv.at[quad * 4 + a]).start()
        pltpu.make_async_copy(v_cols(g), vbuf.at[a, mine], kv_recv.at[quad * 4 + 2 + a]).start()

    barrier = pltpu.get_barrier_semaphore()

    def greet(t):
        pl.semaphore_signal(barrier, inc=1, device_id=t, device_id_type=MESH)

    watch = QUAD - 1
    stand_in = jnp.where(quad == watch, s - 1, s)
    for d in range(1, NYH):
        greet({"seq": stand_in, "batch": lax.rem(yh + d, NYH) * NX + x})
    for d in range(1, NX):
        greet({"seq": stand_in, "batch": yh * NX + lax.rem(x + d, NX)})
    for q in range(QUAD - 1):
        @pl.when(q != quad)
        def _():
            greet(at_seq(z * QUAD + q))

    def greet_z(i, carry):
        t = lax.rem(z + i, NZ) * QUAD + watch

        @pl.when(t != s)
        def _():
            greet(at_seq(t))

        return carry

    lax.fori_loop(0, NZ, greet_z, 0)

    @pl.when(quad < watch - 1)
    def _():
        pl.semaphore_wait(barrier, 9)

    @pl.when(quad == watch - 1)
    def _():
        pl.semaphore_wait(barrier, 15)
        pl.semaphore_signal(plane_sem, inc=1, device_id=at_seq(s + 1), device_id_type=MESH)

    @pl.when(quad == watch)
    def _():
        pl.semaphore_wait(plane_sem, 1)

    copies = []
    for d in (2, 1, 3):
        t = lax.rem(yh + d, NYH)
        copies.append(pltpu.make_async_remote_copy(
            src_ref=w_ref, dst_ref=wbuf.at[yh], send_sem=w_send.at[d], recv_sem=w_recv.at[yh],
            device_id=at_batch(t * NX + x), device_id_type=MESH))
        copies[-1].start()
        t = lax.rem(x + d, NX)
        for j in range(NYH):
            copies.append(pltpu.make_async_remote_copy(
                src_ref=piece(j, t), dst_ref=xbuf.at[j, pl.ds(x * ROWS, ROWS)],
                send_sem=x_send.at[d * NYH + j], recv_sem=x_recv.at[x * NYH + j],
                device_id=at_batch(yh * NX + t), device_id_type=MESH))
            copies[-1].start()

    for a in range(2):
        for d in range(1, QUAD):
            h = lax.rem(quad + d, QUAD)
            g = h + QUAD * a
            for what, (cols, buf) in enumerate(((k_cols, kbuf), (v_cols, vbuf))):
                copies.append(pltpu.make_async_remote_copy(
                    src_ref=cols(g), dst_ref=buf.at[a, mine],
                    send_sem=kv_send.at[d * 4 + what * 2 + a], recv_sem=kv_recv.at[quad * 4 + what * 2 + a],
                    device_id=at_seq(z * QUAD + h), device_id_type=MESH))
                copies[-1].start()

    pos = pos_ref[...]
    last = jnp.minimum(jnp.concatenate([pos, pos], axis=1) + 1, len_ref[0])

    def fill_bias(i, carry):
        row = lax.broadcasted_iota(jnp.int32, (128, 2 * ROWS), 0) + (z * QUAD * KEYS + i * 128)
        bias[pl.ds(pl.multiple_of(i * 128, 128), 128), :] = jnp.where(row < last, 0.0, NEG)
        return carry

    lax.fori_loop(0, QUAD * KEYS // 128, fill_bias, 0)

    for d in range(NYH):
        j = lax.rem(yh + d, NYH)
        arrived(wbuf.at[j], w_recv.at[j])
        for t in range(NX):
            arrived(xbuf.at[j, pl.ds(t * ROWS, ROWS)], x_recv.at[t * NYH + j])
        term = jnp.dot(xbuf[j], wbuf[j], preferred_element_type=jnp.float32)
        if d == 0:
            part[...] = term
        else:
            part[...] += term
    for d in (2, 1, 3):
        t = lax.rem(x + d, NX)
        copies.append(pltpu.make_async_remote_copy(
            src_ref=part.at[pl.ds(t * ROWS, ROWS)], dst_ref=pbuf.at[x],
            send_sem=p_send.at[d], recv_sem=p_recv.at[x],
            device_id=at_batch(yh * NX + t), device_id_type=MESH))
        copies[-1].start()
    pltpu.make_async_copy(part.at[pl.ds(x * ROWS, ROWS)], pbuf.at[x], p_recv.at[x]).start()

    @pl.when(quad == watch)
    def _():
        pl.semaphore_wait(barrier, NZ * QUAD - 1)
        for d in range(1, QUAD):
            pl.semaphore_signal(group_sem, inc=1, device_id=at_seq(s - d), device_id_type=MESH)

    for t in range(NX):
        arrived(pbuf.at[t], p_recv.at[t])
    qown[...] = (pbuf[0] + pbuf[1] + pbuf[2] + pbuf[3]).astype(jnp.bfloat16)

    @pl.when(quad != watch)
    def _():
        pl.semaphore_wait(group_sem, 1)

    my_rows = pl.ds(pl.multiple_of(quad * ROWS, ROWS), ROWS)
    q_slot = unit_of_me * QUAD + quad

    def q_copy(i):
        far = NZ + jnp.where(i % 2 == 1, (i + 1) // 2, -(i // 2))
        t = lax.rem(z + far, NZ) * QUAD + handler
        return t, pltpu.make_async_remote_copy(
            src_ref=qown, dst_ref=qbuf.at[unit_of_me, my_rows], send_sem=q_send.at[i], recv_sem=q_recv.at[q_slot],
            device_id=at_seq(t), device_id_type=MESH)

    def send_q(i, carry):
        t, copy = q_copy(i)

        @pl.when(t != s)
        def _():
            copy.start()

        @pl.when(t == s)
        def _():
            pltpu.make_async_copy(qown, qbuf.at[unit_of_me, my_rows], q_recv.at[q_slot]).start()

        return carry

    lax.fori_loop(0, NZ, send_q, 0)

    def o_copy(u, r):
        t = z_of_unit(u) * QUAD + r
        return t, [
            pltpu.make_async_remote_copy(
                src_ref=src.at[u, r], dst_ref=dst.at[z], send_sem=send.at[u * QUAD + r], recv_sem=recv.at[z],
                device_id=at_seq(t), device_id_type=MESH)
            for src, dst, send, recv in ((outs, ins, t_send, t_recv), (outb, inb, o_send, o_recv))
        ]

    width = QUAD * ROWS

    def attend(u, carry):
        a = u // 2

        @pl.when(u % 2 == 0)
        def _():
            for src in range(QUAD):
                part_rows = pl.ds(src * KEYS, KEYS)
                arrived(kbuf.at[a, part_rows], kv_recv.at[src * 4 + a])
                arrived(vbuf.at[a, part_rows], kv_recv.at[src * 4 + 2 + a])

        for r in range(QUAD):
            arrived(qbuf.at[u, pl.ds(r * ROWS, ROWS)], q_recv.at[u * QUAD + r])
        query = qbuf[u]

        def scores(c, top):
            rows = pl.ds(pl.multiple_of(c * KEYS, KEYS), KEYS)
            raw = lax.dot_general(
                kbuf[a, rows, :], query, (((1,), (1,)), ((), ())), preferred_element_type=jnp.float32
            )
            add = bias[rows, :]
            val = raw * SCALE + jnp.concatenate([add, add], axis=1)
            sbuf[rows, :] = val
            return jnp.maximum(top, jnp.max(val.reshape(KEYS // 8, 8, width), axis=0))

        top = lax.fori_loop(0, QUAD, scores, jnp.full((8, width), -3e38, jnp.float32), unroll=True)
        top = jnp.max(top, axis=0, keepdims=True)

        def weigh(c, carry):
            total, acc = carry
            rows = pl.ds(pl.multiple_of(c * KEYS, KEYS), KEYS)
            expo = jnp.exp2(sbuf[rows, :] - top)
            total = total + jnp.sum(expo.reshape(KEYS // 8, 8, width), axis=0)
            acc = acc + lax.dot_general(
                vbuf[a, rows, :], expo.astype(jnp.bfloat16), (((0,), (0,)), ((), ())),
                preferred_element_type=jnp.float32,
            )
            return total, acc

        total, acc = lax.fori_loop(
            0, QUAD, weigh,
            (jnp.zeros((8, width), jnp.float32), jnp.zeros((HD, width), jnp.float32)), unroll=True,
        )
        total = jnp.sum(total, axis=0, keepdims=True)

        for half in range(2):
            block = acc[:, half * 128:(half + 1) * 128].T.astype(jnp.bfloat16)
            for r in range(2):
                outb[u, half * 2 + r] = block[r * ROWS:(r + 1) * ROWS]
                outs[u, half * 2 + r, 0:1, :] = top[:, half * 128:(half + 1) * 128]
                outs[u, half * 2 + r, 1:2, :] = total[:, half * 128:(half + 1) * 128]
        for r in range(QUAD):
            t, pair = o_copy(u, r)

            @pl.when(t != s)
            def _():
                for copy in pair:
                    copy.start()

            @pl.when(t == s)
            def _():
                pltpu.make_async_copy(outb.at[u, r], inb.at[z], o_recv.at[z]).start()
                pltpu.make_async_copy(outs.at[u, r], ins.at[z], t_recv.at[z]).start()

        return carry

    lax.fori_loop(0, UNITS, attend, 0)

    maxima, totals = [], []
    for i in range(NZ):
        arrived(ins.at[i], t_recv.at[i])
        maxima.append(ins[i, 0:1, :])
        totals.append(ins[i, 1:2, :])
    top = functools.reduce(jnp.maximum, maxima)
    weights = [jnp.exp2(m - top) for m in maxima]
    denom = functools.reduce(jnp.add, [w * t for w, t in zip(weights, totals)])
    inverse = 1.0 / denom
    sub = lax.broadcasted_iota(jnp.int32, (128, 128), 0)
    table = jnp.zeros((128, 128), jnp.float32)
    for i in range(NZ):
        table = jnp.where(sub == i, weights[i] * inverse, table)
    coef[...] = table.T
    mine_rows = pl.ds(pl.multiple_of((quad % 2) * ROWS, ROWS), ROWS)
    cols = coef[mine_rows, :]
    result = jnp.zeros((ROWS, HD), jnp.float32)
    for i in range(NZ):
        arrived(inb.at[i], o_recv.at[i])
        result = result + cols[:, i:i + 1] * inb[i].astype(jnp.float32)
    o_ref[0] = result.astype(jnp.bfloat16)

    for copy in copies:
        copy.wait_send()

    def left(i, carry):
        t, copy = q_copy(i)

        @pl.when(t != s)
        def _():
            copy.wait_send()

        t2, copy2 = o_copy(i // QUAD, i % QUAD)

        @pl.when(t2 != s)
        def _():
            for one in copy2:
                one.wait_send()

        return carry

    lax.fori_loop(0, NZ, left, 0)


def on_device(inputs, w_query, cache_keys, cache_values, lengths, positions):
    any_spec = pl.BlockSpec(memory_space=pl.ANY)
    bf, f32 = jnp.bfloat16, jnp.float32
    dma = pltpu.SemaphoreType.DMA
    return pl.pallas_call(
        kernel,
        out_shape=jax.ShapeDtypeStruct((1, ROWS, HD), bf),
        in_specs=[any_spec] * 4 + [pl.BlockSpec(memory_space=pltpu.SMEM), pl.BlockSpec(memory_space=pltpu.VMEM)],
        out_specs=pl.BlockSpec(memory_space=pltpu.VMEM),
        scratch_shapes=[
            pltpu.VMEM((NYH, DEPTH, HD), bf),
            pltpu.VMEM((NYH, NX * ROWS, DEPTH), bf),
            pltpu.VMEM((NX * ROWS, HD), f32),
            pltpu.VMEM((NX, ROWS, HD), f32),
            pltpu.VMEM((ROWS, HD), bf),
            pltpu.VMEM((UNITS, QUAD * ROWS, HD), bf),
            pltpu.VMEM((2, QUAD * KEYS, HD), bf),
            pltpu.VMEM((2, QUAD * KEYS, HD), bf),
            pltpu.VMEM((QUAD * KEYS, 2 * ROWS), f32),
            pltpu.VMEM((QUAD * KEYS, QUAD * ROWS), f32),
            pltpu.VMEM((UNITS, QUAD, ROWS, HD), bf),
            pltpu.VMEM((NZ, ROWS, HD), bf),
            pltpu.VMEM((UNITS, QUAD, 2, 128), f32),
            pltpu.VMEM((NZ, 2, 128), f32),
            pltpu.VMEM((128, 128), f32),
            dma((NYH,)), dma((NYH,)),
            dma((NX * NYH,)), dma((NX * NYH,)),
            dma((QUAD * 4,)), dma((QUAD * 4,)),
            dma((NX,)), dma((NX,)),
            dma((NZ,)), dma((NZ,)),
            dma((NZ,)), dma((NZ,)),
            dma((NZ,)), dma((NZ,)),
            pltpu.SemaphoreType.REGULAR, pltpu.SemaphoreType.REGULAR,
        ],
        compiler_params=pltpu.CompilerParams(
            collective_id=0, has_side_effects=True, vmem_limit_bytes=40 * 2**20
        ),
    )(inputs, w_query, cache_keys, cache_values, lengths, positions)


def solution(mesh):
    in_specs = (
        P("batch", None, None),
        P("batch", "seq"),
        P("batch", "seq", None),
        P("batch", "seq", None),
        P("batch"),
        P("batch", None),
    )
    return jax.shard_map(
        on_device, mesh=mesh, in_specs=in_specs, out_specs=P("batch", None, "seq"), check_vma=False
    )
```

```python
import functools
import jax
import jax.numpy as jnp
from jax import lax
from jax.experimental import pallas as pl
from jax.experimental.pallas import tpu as pltpu
from jax.sharding import PartitionSpec as P

MESH = pl.DeviceIdType.MESH
HD = 128
QUAD = 4
NX = 4
NYH = 4
NZ = 16
UNITS = 4
ROWS = 64
DEPTH = 512
KEYS = 512
SCALE = HD ** (-0.5) * 1.4426950408889634
NEG = -1e30


def arrived(ref, sem):
    pltpu.make_async_copy(ref, ref, sem).wait()


def kernel(
    x_ref, w_ref, k_ref, v_ref, len_ref, pos_ref, o_ref,
    wbuf, xbuf, part, pbuf, qown, qbuf, kbuf, vbuf, bias, sbuf, outb, inb, outs, ins, coef,
    w_send, w_recv, x_send, x_recv, kv_send, kv_recv, p_send, p_recv, q_send, q_recv, o_send, o_recv, t_send, t_recv,
    plane_sem, group_sem,
):
    s = lax.axis_index("seq")
    b = lax.axis_index("batch")
    z, quad = s // QUAD, s % QUAD
    yh, x = b // NX, b % NX
    unit_of_me = 2 * (z // 8) + z % 2
    handler = (z // 2) % QUAD

    def at_seq(t):
        return {"seq": t, "batch": b}

    def at_batch(t):
        return {"seq": s, "batch": t}

    def z_of_unit(u):
        return 2 * quad + 8 * (u // 2) + u % 2

    def piece(j, xt):
        return x_ref.at[0, :, pl.ds(pl.multiple_of((j * NX + xt) * DEPTH, DEPTH), DEPTH)]

    def k_cols(g):
        return k_ref.at[0, :, pl.ds(pl.multiple_of(g * HD, HD), HD)]

    def v_cols(g):
        return v_ref.at[0, :, pl.ds(pl.multiple_of(g * HD, HD), HD)]

    mine = pl.ds(pl.multiple_of(quad * KEYS, KEYS), KEYS)

    pltpu.make_async_copy(w_ref, wbuf.at[yh], w_recv.at[yh]).start()
    for j in range(NYH):
        pltpu.make_async_copy(piece(j, x), xbuf.at[j, pl.ds(x * ROWS, ROWS)], x_recv.at[x * NYH + j]).start()
    for a in range(2):
        g = quad + QUAD * a
        pltpu.make_async_copy(k_cols(g), kbuf.at[a, mine], kv_recv.at[quad * 4 + a]).start()
        pltpu.make_async_copy(v_cols(g), vbuf.at[a, mine], kv_recv.at[quad * 4 + 2 + a]).start()

    barrier = pltpu.get_barrier_semaphore()

    def greet(t):
        pl.semaphore_signal(barrier, inc=1, device_id=t, device_id_type=MESH)

    watch = QUAD - 1
    stand_in = jnp.where(quad == watch, s - 1, s)
    for d in range(1, NYH):
        greet({"seq": stand_in, "batch": lax.rem(yh + d, NYH) * NX + x})
    for d in range(1, NX):
        greet({"seq": stand_in, "batch": yh * NX + lax.rem(x + d, NX)})
    for q in range(QUAD - 1):
        @pl.when(q != quad)
        def _():
            greet(at_seq(z * QUAD + q))

    def greet_z(i, carry):
        t = lax.rem(z + i, NZ) * QUAD + watch

        @pl.when(t != s)
        def _():
            greet(at_seq(t))

        return carry

    lax.fori_loop(0, NZ, greet_z, 0)

    @pl.when(quad < watch - 1)
    def _():
        pl.semaphore_wait(barrier, 9)

    @pl.when(quad == watch - 1)
    def _():
        pl.semaphore_wait(barrier, 15)
        pl.semaphore_signal(plane_sem, inc=1, device_id=at_seq(s + 1), device_id_type=MESH)

    @pl.when(quad == watch)
    def _():
        pl.semaphore_wait(plane_sem, 1)

    copies = []
    for d in (2, 1, 3):
        t = lax.rem(yh + d, NYH)
        copies.append(pltpu.make_async_remote_copy(
            src_ref=w_ref, dst_ref=wbuf.at[yh], send_sem=w_send.at[d], recv_sem=w_recv.at[yh],
            device_id=at_batch(t * NX + x), device_id_type=MESH))
        copies[-1].start()
        t = lax.rem(x + d, NX)
        for j in range(NYH):
            copies.append(pltpu.make_async_remote_copy(
                src_ref=piece(j, t), dst_ref=xbuf.at[j, pl.ds(x * ROWS, ROWS)],
                send_sem=x_send.at[d * NYH + j], recv_sem=x_recv.at[x * NYH + j],
                device_id=at_batch(yh * NX + t), device_id_type=MESH))
            copies[-1].start()

    for a in range(2):
        for d in range(1, QUAD):
            h = lax.rem(quad + d, QUAD)
            g = h + QUAD * a
            for what, (cols, buf) in enumerate(((k_cols, kbuf), (v_cols, vbuf))):
                copies.append(pltpu.make_async_remote_copy(
                    src_ref=cols(g), dst_ref=buf.at[a, mine],
                    send_sem=kv_send.at[d * 4 + what * 2 + a], recv_sem=kv_recv.at[quad * 4 + what * 2 + a],
                    device_id=at_seq(z * QUAD + h), device_id_type=MESH))
                copies[-1].start()

    pos = pos_ref[...]
    last = jnp.minimum(jnp.concatenate([pos, pos], axis=1) + 1, len_ref[0])

    def fill_bias(i, carry):
        row = lax.broadcasted_iota(jnp.int32, (128, 2 * ROWS), 0) + (z * QUAD * KEYS + i * 128)
        bias[pl.ds(pl.multiple_of(i * 128, 128), 128), :] = jnp.where(row < last, 0.0, NEG)
        return carry

    lax.fori_loop(0, QUAD * KEYS // 128, fill_bias, 0)

    for d in range(NYH):
        j = lax.rem(yh + d, NYH)
        arrived(wbuf.at[j], w_recv.at[j])
        for t in range(NX):
            arrived(xbuf.at[j, pl.ds(t * ROWS, ROWS)], x_recv.at[t * NYH + j])
        term = jnp.dot(xbuf[j], wbuf[j], preferred_element_type=jnp.float32)
        if d == 0:
            part[...] = term
        else:
            part[...] += term
    for d in (2, 1, 3):
        t = lax.rem(x + d, NX)
        copies.append(pltpu.make_async_remote_copy(
            src_ref=part.at[pl.ds(t * ROWS, ROWS)], dst_ref=pbuf.at[x],
            send_sem=p_send.at[d], recv_sem=p_recv.at[x],
            device_id=at_batch(yh * NX + t), device_id_type=MESH))
        copies[-1].start()
    pltpu.make_async_copy(part.at[pl.ds(x * ROWS, ROWS)], pbuf.at[x], p_recv.at[x]).start()

    @pl.when(quad == watch)
    def _():
        pl.semaphore_wait(barrier, NZ * QUAD - 1)
        for d in range(1, QUAD):
            pl.semaphore_signal(group_sem, inc=1, device_id=at_seq(s - d), device_id_type=MESH)

    for t in range(NX):
        arrived(pbuf.at[t], p_recv.at[t])
    qown[...] = (pbuf[0] + pbuf[1] + pbuf[2] + pbuf[3]).astype(jnp.bfloat16)

    @pl.when(quad != watch)
    def _():
        pl.semaphore_wait(group_sem, 1)

    my_rows = pl.ds(pl.multiple_of(quad * ROWS, ROWS), ROWS)
    q_slot = unit_of_me * QUAD + quad

    def q_copy(i):
        half = NZ // 2
        t = (half * (i // half) + lax.rem(z + i, half)) * QUAD + handler
        return t, pltpu.make_async_remote_copy(
            src_ref=qown, dst_ref=qbuf.at[unit_of_me, my_rows], send_sem=q_send.at[i], recv_sem=q_recv.at[q_slot],
            device_id=at_seq(t), device_id_type=MESH)

    def send_q(i, carry):
        t, copy = q_copy(i)

        @pl.when(t != s)
        def _():
            copy.start()

        @pl.when(t == s)
        def _():
            pltpu.make_async_copy(qown, qbuf.at[unit_of_me, my_rows], q_recv.at[q_slot]).start()

        return carry

    lax.fori_loop(0, NZ, send_q, 0)

    def o_copy(u, r):
        t = z_of_unit(u) * QUAD + r
        return t, [
            pltpu.make_async_remote_copy(
                src_ref=src.at[u, r], dst_ref=dst.at[z], send_sem=send.at[u * QUAD + r], recv_sem=recv.at[z],
                device_id=at_seq(t), device_id_type=MESH)
            for src, dst, send, recv in ((outs, ins, t_send, t_recv), (outb, inb, o_send, o_recv))
        ]

    width = QUAD * ROWS

    def attend(u, carry):
        a = u // 2

        @pl.when(u % 2 == 0)
        def _():
            for src in range(QUAD):
                part_rows = pl.ds(src * KEYS, KEYS)
                arrived(kbuf.at[a, part_rows], kv_recv.at[src * 4 + a])
                arrived(vbuf.at[a, part_rows], kv_recv.at[src * 4 + 2 + a])

        for r in range(QUAD):
            arrived(qbuf.at[u, pl.ds(r * ROWS, ROWS)], q_recv.at[u * QUAD + r])
        query = qbuf[u]

        def scores(c, top):
            rows = pl.ds(pl.multiple_of(c * KEYS, KEYS), KEYS)
            raw = lax.dot_general(
                kbuf[a, rows, :], query, (((1,), (1,)), ((), ())), preferred_element_type=jnp.float32
            )
            add = bias[rows, :]
            val = raw * SCALE + jnp.concatenate([add, add], axis=1)
            sbuf[rows, :] = val
            return jnp.maximum(top, jnp.max(val.reshape(KEYS // 8, 8, width), axis=0))

        top = lax.fori_loop(0, QUAD, scores, jnp.full((8, width), -3e38, jnp.float32), unroll=True)
        top = jnp.max(top, axis=0, keepdims=True)

        def weigh(c, carry):
            total, acc = carry
            rows = pl.ds(pl.multiple_of(c * KEYS, KEYS), KEYS)
            expo = jnp.exp2(sbuf[rows, :] - top)
            total = total + jnp.sum(expo.reshape(KEYS // 8, 8, width), axis=0)
            acc = acc + lax.dot_general(
                vbuf[a, rows, :], expo.astype(jnp.bfloat16), (((0,), (0,)), ((), ())),
                preferred_element_type=jnp.float32,
            )
            return total, acc

        total, acc = lax.fori_loop(
            0, QUAD, weigh,
            (jnp.zeros((8, width), jnp.float32), jnp.zeros((HD, width), jnp.float32)), unroll=True,
        )
        total = jnp.sum(total, axis=0, keepdims=True)

        for half in range(2):
            block = acc[:, half * 128:(half + 1) * 128].T.astype(jnp.bfloat16)
            for r in range(2):
                outb[u, half * 2 + r] = block[r * ROWS:(r + 1) * ROWS]
                outs[u, half * 2 + r, 0:1, :] = top[:, half * 128:(half + 1) * 128]
                outs[u, half * 2 + r, 1:2, :] = total[:, half * 128:(half + 1) * 128]
        for r in range(QUAD):
            t, pair = o_copy(u, r)

            @pl.when(t != s)
            def _():
                for copy in pair:
                    copy.start()

            @pl.when(t == s)
            def _():
                pltpu.make_async_copy(outb.at[u, r], inb.at[z], o_recv.at[z]).start()
                pltpu.make_async_copy(outs.at[u, r], ins.at[z], t_recv.at[z]).start()

        return carry

    lax.fori_loop(0, UNITS, attend, 0)

    maxima, totals = [], []
    for i in range(NZ):
        arrived(ins.at[i], t_recv.at[i])
        maxima.append(ins[i, 0:1, :])
        totals.append(ins[i, 1:2, :])
    top = functools.reduce(jnp.maximum, maxima)
    weights = [jnp.exp2(m - top) for m in maxima]
    denom = functools.reduce(jnp.add, [w * t for w, t in zip(weights, totals)])
    inverse = 1.0 / denom
    sub = lax.broadcasted_iota(jnp.int32, (128, 128), 0)
    table = jnp.zeros((128, 128), jnp.float32)
    for i in range(NZ):
        table = jnp.where(sub == i, weights[i] * inverse, table)
    coef[...] = table.T
    mine_rows = pl.ds(pl.multiple_of((quad % 2) * ROWS, ROWS), ROWS)
    cols = coef[mine_rows, :]
    result = jnp.zeros((ROWS, HD), jnp.float32)
    for i in range(NZ):
        arrived(inb.at[i], o_recv.at[i])
        result = result + cols[:, i:i + 1] * inb[i].astype(jnp.float32)
    o_ref[0] = result.astype(jnp.bfloat16)

    for copy in copies:
        copy.wait_send()

    def left(i, carry):
        t, copy = q_copy(i)

        @pl.when(t != s)
        def _():
            copy.wait_send()

        t2, copy2 = o_copy(i // QUAD, i % QUAD)

        @pl.when(t2 != s)
        def _():
            for one in copy2:
                one.wait_send()

        return carry

    lax.fori_loop(0, NZ, left, 0)


def on_device(inputs, w_query, cache_keys, cache_values, lengths, positions):
    any_spec = pl.BlockSpec(memory_space=pl.ANY)
    bf, f32 = jnp.bfloat16, jnp.float32
    dma = pltpu.SemaphoreType.DMA
    return pl.pallas_call(
        kernel,
        out_shape=jax.ShapeDtypeStruct((1, ROWS, HD), bf),
        in_specs=[any_spec] * 4 + [pl.BlockSpec(memory_space=pltpu.SMEM), pl.BlockSpec(memory_space=pltpu.VMEM)],
        out_specs=pl.BlockSpec(memory_space=pltpu.VMEM),
        scratch_shapes=[
            pltpu.VMEM((NYH, DEPTH, HD), bf),
            pltpu.VMEM((NYH, NX * ROWS, DEPTH), bf),
            pltpu.VMEM((NX * ROWS, HD), f32),
            pltpu.VMEM((NX, ROWS, HD), f32),
            pltpu.VMEM((ROWS, HD), bf),
            pltpu.VMEM((UNITS, QUAD * ROWS, HD), bf),
            pltpu.VMEM((2, QUAD * KEYS, HD), bf),
            pltpu.VMEM((2, QUAD * KEYS, HD), bf),
            pltpu.VMEM((QUAD * KEYS, 2 * ROWS), f32),
            pltpu.VMEM((QUAD * KEYS, QUAD * ROWS), f32),
            pltpu.VMEM((UNITS, QUAD, ROWS, HD), bf),
            pltpu.VMEM((NZ, ROWS, HD), bf),
            pltpu.VMEM((UNITS, QUAD, 2, 128), f32),
            pltpu.VMEM((NZ, 2, 128), f32),
            pltpu.VMEM((128, 128), f32),
            dma((NYH,)), dma((NYH,)),
            dma((NX * NYH,)), dma((NX * NYH,)),
            dma((QUAD * 4,)), dma((QUAD * 4,)),
            dma((NX,)), dma((NX,)),
            dma((NZ,)), dma((NZ,)),
            dma((NZ,)), dma((NZ,)),
            dma((NZ,)), dma((NZ,)),
            pltpu.SemaphoreType.REGULAR, pltpu.SemaphoreType.REGULAR,
        ],
        compiler_params=pltpu.CompilerParams(
            collective_id=0, has_side_effects=True, vmem_limit_bytes=40 * 2**20
        ),
    )(inputs, w_query, cache_keys, cache_values, lengths, positions)


def solution(mesh):
    in_specs = (
        P("batch", None, None),
        P("batch", "seq"),
        P("batch", "seq", None),
        P("batch", "seq", None),
        P("batch"),
        P("batch", None),
    )
    return jax.shard_map(
        on_device, mesh=mesh, in_specs=in_specs, out_specs=P("batch", None, "seq"), check_vma=False
    )
```
